1024 devices in a mesh: blk: 128 (over z_lo, x, core), grp: 8 (over z_hi, y).
Axes of the slice: x: 4, y: 4, z: 32 (z_hi: 2, z_lo: 16; z = z_hi * 16 + z_lo), core: 2. Of those that a mesh axis runs over, the one named last changes fastest.
Arguments:
- image_emb: bfloat16 [131072, 1152], P(('blk', 'grp')), may hold values from -0.19921875 to 0.19921875
- text_emb: bfloat16 [131072, 1152], P(('blk', 'grp')), may hold values from -0.19921875 to 0.19921875
- loop_mask: int32 [1024, 4], P(('blk', 'grp')), may hold values from 0 to 1, as said below
- neg_list: int32 [1024, 2], P(('blk', 'grp')), may hold values from 0 to 7, as said below
Outputs:
- row_loss: float32 [131072], P(('blk', 'grp'))
- image_grad: bfloat16 [131072, 1152], P(('blk', 'grp'))
- text_grad: bfloat16 [131072, 1152], P(('blk', 'grp'))
The draws below stay inside these ranges and needn't reach their ends.
Inputs may be any that keep to these rules, and one draw needn't show every extreme that they name: `loop_mask`: 1 marks a scored pair of blocks, 0 an unscored one. `neg_list`: the 2 entries of a row are distinct and differ from the row's own group index, k mod 8.
All inputs are finite; a program needn't handle non-finite values.
Results may differ from the reference program's by a relative error of at most 0.013.
Values may be sent and summed in bfloat16 or wider, within the bound.
A program may use at most 32 MiB of HBM per device.

```python
import jax
import jax.numpy as jnp
from jax import lax

D = 1152
ROWS = 128
HALF = 2
KNEG = 2
CYCLE = 128
GROUP = 8
NBLK = 1024
BATCH = 131072


def draw_loop_mask(key, part):
    key = jax.random.fold_in(key, 11)
    level_key, bits_key = jax.random.split(key)
    level = jax.random.randint(level_key, (NBLK, 1), 1, 5)
    bits = jax.random.randint(bits_key, (NBLK, 2 * HALF), 0, 4)
    return (bits < level).astype(jnp.int32)


def draw_neg_list(key, part):
    key = jax.random.fold_in(key, 12)
    first_key, second_key = jax.random.split(key)
    first = jax.random.randint(first_key, (NBLK,), 1, GROUP)
    second = jax.random.randint(second_key, (NBLK,), 1, GROUP - 1)
    second = second + (second >= first).astype(jnp.int32)
    own_group = jnp.arange(NBLK, dtype=jnp.int32) % GROUP
    picks = jnp.stack([(own_group + first) % GROUP, (own_group + second) % GROUP], axis=1)
    return picks.astype(jnp.int32)


def block_scale(stream_key, extent, shards, low, high):
    loudness, own = 1.0, jax.random.fold_in(stream_key, 6)
    for position, parts in shards:
        draws = jnp.exp(jax.random.uniform(jax.random.fold_in(own, position), (parts,), jnp.float32, low / len(shards), high / len(shards)))
        loudness = loudness * jnp.repeat(draws, extent[position] // parts).reshape([-1 if axis == position else 1 for axis in range(len(extent))])
    return loudness


def centred(stream_key, shape, deviation, reach, pieces=(), kind=jnp.bfloat16):
    entries = deviation * jax.random.normal(stream_key, shape, jnp.float32)
    if pieces:
        entries = entries * block_scale(stream_key, shape, pieces, -0.22, 0.18)
    return jnp.clip(entries, -reach, reach).astype(kind)


def setup_inputs(seed: int = 0) -> dict:
    streams_of = jax.random.split(jax.random.key(seed), 5)
    return {
        "image_emb": centred(streams_of[0], (BATCH, D), 0.03, 0.19921875, ((0, 1024),)),
        "text_emb": centred(streams_of[1], (BATCH, D), 0.03, 0.19921875, ((0, 1024),)),
        "loop_mask": draw_loop_mask(jax.random.fold_in(streams_of[4], 71), 0),
        "neg_list": draw_neg_list(jax.random.fold_in(streams_of[4], 71), 0),
    }


epsilon = 1e-06
logit_scale = 16.0
logit_bias = -2.0

def normalize(embedding):
    values = embedding.astype(jnp.float32)
    magnitude = jnp.sqrt(lax.optimization_barrier(jnp.sum(values * values, axis=-1, keepdims=True)) + epsilon)
    unit_full = values / magnitude
    return (magnitude, unit_full, unit_full.astype(jnp.bfloat16))

def unit_backward(unit_full, magnitude, unit_grad):
    along = lax.optimization_barrier(jnp.sum(unit_full * unit_grad, axis=-1, keepdims=True))
    return ((unit_grad - unit_full * along) / magnitude).astype(jnp.bfloat16)

def pair_terms(image_blocks, text_blocks, weight, own_block):
    image_wide = image_blocks.astype(jnp.float32)
    text_wide = text_blocks.astype(jnp.float32)
    scores = logit_scale * jnp.einsum('nrd,ncd->nrc', image_wide, text_wide) + logit_bias
    pair_grad = jax.nn.sigmoid(scores)
    losses = lax.optimization_barrier(jnp.sum(jax.nn.softplus(scores), axis=-1))
    if own_block:
        pair_grad = pair_grad - jnp.eye(scores.shape[1], dtype=jnp.float32)
        losses = losses - jnp.diagonal(scores, axis1=1, axis2=2)
    pair_grad = pair_grad * weight[:, None, None]
    losses = losses * weight[:, None]
    grad_half = lax.optimization_barrier(pair_grad.astype(jnp.bfloat16)).astype(jnp.float32)
    image_part = logit_scale * jnp.einsum('nrc,ncd->nrd', grad_half, text_wide)
    text_part = logit_scale * jnp.einsum('nrc,nrd->ncd', grad_half, image_wide)
    return (losses, image_part, text_part)

def reference(image_emb, text_emb, loop_mask, neg_list):
    image_mag, image_full, image_unit = normalize(image_emb)
    text_mag, text_full, text_unit = normalize(text_emb)
    image_blocks = image_unit.reshape(NBLK, ROWS, D)
    text_blocks = text_unit.reshape(NBLK, ROWS, D)
    text_loop = text_unit.reshape(CYCLE, GROUP, ROWS, D)
    all_ones = jnp.ones((NBLK,), jnp.float32)
    losses, image_total, text_total = pair_terms(image_blocks, text_blocks, all_ones, True)
    offsets = list(range(-HALF, 0)) + list(range(1, HALF + 1))
    for offset in offsets:
        mask_col = offset + HALF if offset < 0 else offset + HALF - 1
        visitor = jnp.roll(text_loop, -offset, axis=0).reshape(NBLK, ROWS, D)
        weight = loop_mask[:, mask_col].astype(jnp.float32)
        part_loss, image_part, text_part = pair_terms(image_blocks, visitor, weight, False)
        losses = losses + part_loss
        image_total = image_total + image_part
        text_back = jnp.roll(text_part.reshape(CYCLE, GROUP, ROWS, D), offset, axis=0)
        text_total = text_total + text_back.reshape(NBLK, ROWS, D)
    base_ids = jnp.arange(NBLK, dtype=jnp.int32) // GROUP * GROUP
    for pick in range(KNEG):
        block_ids = (base_ids + neg_list[:, pick]).astype(jnp.int32)
        fetched = text_blocks[block_ids]
        part_loss, image_part, text_part = pair_terms(image_blocks, fetched, all_ones, False)
        losses = losses + part_loss
        image_total = image_total + image_part
        rounded = lax.optimization_barrier(text_part.astype(jnp.bfloat16)).astype(jnp.float32)
        text_total = text_total.at[block_ids].add(rounded)
    row_loss = losses.reshape(BATCH)
    image_grad = unit_backward(image_full, image_mag, image_total.reshape(BATCH, D))
    text_grad = unit_backward(text_full, text_mag, text_total.reshape(BATCH, D))
    return (row_loss, image_grad, text_grad)
```

```python
import jax
import jax.numpy as jnp
from jax import lax
from jax.experimental import pallas as pl
from jax.experimental.pallas import tpu as pltpu
from jax.sharding import PartitionSpec as P

MESH = pl.DeviceIdType.MESH

epsilon = 1e-06
logit_scale = 16.0
logit_bias = -2.0

PIECES = 4
STEPS = 2 * PIECES
AHEAD = 3
OWN = 4
FAR = 8


def normalize_rows(emb_ref, mag_ref, unit_ref, first):
    rows = emb_ref.shape[0]

    def some(i, carry):
        at = pl.ds(pl.multiple_of(i * 16, 16), 16)
        values = emb_ref[at, :].astype(jnp.float32)
        magnitude = jnp.sqrt(jnp.sum(values * values, axis=-1, keepdims=True) + epsilon)
        mag_ref[at, :] = magnitude
        unit = (values / magnitude).astype(jnp.bfloat16)
        unit_ref[pl.ds(pl.multiple_of(first + i * 16, 16), 16), :] = unit
        return carry

    lax.fori_loop(0, rows // 16, some, 0)


def backward_rows(emb_ref, mag_ref, sum_ref, out_ref):
    rows = emb_ref.shape[0]

    def some(i, carry):
        at = pl.ds(pl.multiple_of(i * 16, 16), 16)
        magnitude = mag_ref[at, :]
        full = emb_ref[at, :].astype(jnp.float32) / magnitude
        grad = logit_scale * sum_ref[at, :]
        along = jnp.sum(full * grad, axis=-1, keepdims=True)
        out_ref[at, :] = ((grad - full * along) / magnitude).astype(jnp.bfloat16)
        return carry

    lax.fori_loop(0, rows // 16, some, 0)


def kernel(
    image_ref, text_ref, mask_ref, neg_ref,
    loss_ref, image_out, text_out,
    own, held, tiles, image_mag, text_mag, image_sum, text_sum, loss_sum,
    far_send, far_recv, slot_send, slot_recv, tile_send, tile_recv, pass_send, pass_recv,
):
    rows = image_ref.shape[0]
    part = rows // PIECES
    p = lax.axis_index("blk")
    g = lax.axis_index("grp")
    n = lax.axis_size("blk")
    half, y = g // 4, lax.rem(g, 4)
    core = lax.rem(p, 2)

    def near(dy):
        return (p, half * 4 + lax.rem(y + dy, 4))

    far = (p, lax.rem(g + 4, 8))
    after = (lax.rem(p + 2, n), g)
    before = (lax.rem(p + n - 2, n), g)
    twin = (p + 1 - 2 * core, g)
    partners = [far, after, before, twin, near(1), near(2), near(3)]

    barrier = pltpu.get_barrier_semaphore()
    for device in partners:
        pl.semaphore_signal(barrier, inc=1, device_id=device, device_id_type=MESH)

    lane = lax.broadcasted_iota(jnp.int32, (8, 128), 1)
    mine = (lane == neg_ref[0, 0]) | (lane == neg_ref[0, 1]) | (lane == g)
    tile = jnp.where(mine, 1.0, 0.0)
    for k in range(4):
        tile = jnp.where(lane == 8 + k, mask_ref[0, k].astype(jnp.float32), tile)
    tiles[OWN] = tile
    normalize_rows(text_ref, text_mag, own, 0)
    normalize_rows(image_ref, image_mag, own, rows)
    held[OWN] = own[...]
    image_sum[...] = jnp.zeros_like(image_sum)
    text_sum[...] = jnp.zeros_like(text_sum)
    loss_sum[...] = jnp.zeros_like(loss_sum)

    def far_copy(j):
        at = pl.ds(pl.multiple_of(j * part, part), part)
        return pltpu.make_async_remote_copy(
            src_ref=own.at[at], dst_ref=held.at[FAR, at],
            send_sem=far_send.at[j], recv_sem=far_recv.at[j],
            device_id=far, device_id_type=MESH,
        )

    def slot_copy(i, src, slot, device):
        return pltpu.make_async_remote_copy(
            src_ref=src, dst_ref=held.at[slot],
            send_sem=slot_send.at[i], recv_sem=slot_recv.at[slot],
            device_id=device, device_id_type=MESH,
        )

    def tile_copy(i, src_slot, slot, device):
        return pltpu.make_async_remote_copy(
            src_ref=tiles.at[src_slot], dst_ref=tiles.at[slot],
            send_sem=tile_send.at[i], recv_sem=tile_recv.at[slot],
            device_id=device, device_id_type=MESH,
        )

    def pass_copy(dy, j):
        at = pl.ds(pl.multiple_of(j * part, part), part)
        return pltpu.make_async_remote_copy(
            src_ref=held.at[FAR, at], dst_ref=held.at[FAR + 4 - dy, at],
            send_sem=pass_send.at[dy - 1, j], recv_sem=pass_recv.at[3 - dy, j],
            device_id=near(dy), device_id_type=MESH,
        )

    pl.semaphore_wait(barrier, len(partners))

    for j in range(AHEAD):
        far_copy(j).start()
    targets = [(after, 0), (before, 3), (twin, 1 + core)] + [(near(dy), OWN + 4 - dy) for dy in (1, 2, 3)]
    for i, (device, slot) in enumerate(targets):
        tile_copy(i, OWN, slot, device).start()
    tile_copy(6, OWN, FAR, far).start()
    for i, (device, slot) in enumerate(targets):
        slot_copy(i, own, slot, device).start()

    source, place = 3 - 3 * core, 2 - core
    tile_copy(7, source, source, twin).wait_recv()
    tile_copy(7, source, place, twin).start()
    slot_copy(6, held.at[source], source, twin).wait_recv()
    slot_copy(6, held.at[source], place, twin).start()
    tile_copy(6, FAR, FAR, far).wait_recv()
    for dy in (1, 2, 3):
        tile_copy(7 + dy, FAR, FAR + 4 - dy, near(dy)).start()

    row = lax.broadcasted_iota(jnp.int32, (rows, rows), 0)
    column = lax.broadcasted_iota(jnp.int32, (rows, rows), 1)
    eye = jnp.where(row == column, 1.0, 0.0)
    first_lane = lax.broadcasted_iota(jnp.int32, (1, 128), 1)

    def weight(slot, index):
        picked = jnp.where(first_lane == index, tiles[slot, 0:1, :], 0.0)
        return jnp.sum(picked, axis=1, keepdims=True)

    def scores_of(own_block, other):
        return logit_scale * lax.dot_general(
            own_block, other, (((1,), (1,)), ((), ())), preferred_element_type=jnp.float32
        ) + logit_bias

    def image_side(slot, index, diagonal):
        other = held[slot, pl.ds(0, rows), :]
        scores = scores_of(own[pl.ds(rows, rows), :], other)
        w = weight(OWN, index)
        small = jnp.exp(-jnp.abs(scores))
        loss = jnp.maximum(scores, 0.0) + jnp.log1p(small)
        grad = jnp.where(scores >= 0.0, 1.0, small) / (1.0 + small)
        if diagonal is not None:
            loss = loss - diagonal * scores
            grad = grad - diagonal
        loss_sum[...] += w * loss
        image_sum[...] += jnp.dot(
            (w * grad).astype(jnp.bfloat16), other, preferred_element_type=jnp.float32
        )

    def text_side(slot, index, diagonal):
        other = held[slot, pl.ds(rows, rows), :]
        scores = scores_of(own[pl.ds(0, rows), :], other)
        w = weight(slot, index)
        small = jnp.exp(-jnp.abs(scores))
        grad = jnp.where(scores >= 0.0, 1.0, small) / (1.0 + small)
        if diagonal is not None:
            grad = grad - diagonal
        text_sum[...] += jnp.dot(
            (w * grad).astype(jnp.bfloat16), other, preferred_element_type=jnp.float32
        )

    def step(j, carry):
        far_copy(j).wait_recv()
        for dy in (1, 2, 3):
            pass_copy(dy, j).start()
        far_copy(j).wait_send()

        @pl.when(j < STEPS - AHEAD)
        def _():
            far_copy(j + AHEAD).start()

        @pl.when((j != OWN) & (j != source))
        def _():
            slot_copy(0, own, j, after).wait_recv()
            tile_copy(0, OWN, j, after).wait_recv()

        in_loop = j < 4
        group_index = half * 4 + lax.rem(y + j, 4)
        diagonal = jnp.where(j == OWN, 1.0, 0.0) * eye
        image_side(j, jnp.where(in_loop, 8 + j, group_index), diagonal)
        text_side(j, jnp.where(in_loop, 11 - j, g), diagonal)

        @pl.when(j >= 4)
        def _():
            @pl.when(j > 4)
            def _():
                def arrived(k, c):
                    at = pl.ds(pl.multiple_of(k * part, part), part)
                    pltpu.make_async_remote_copy(
                        src_ref=own.at[at], dst_ref=held.at[j + 4, at],
                        send_sem=far_send.at[k], recv_sem=pass_recv.at[j - 5, k],
                        device_id=far, device_id_type=MESH,
                    ).wait_recv()
                    return c
                lax.fori_loop(0, PIECES, arrived, 0)

            image_side(j + 4, (1 - half) * 4 + lax.rem(y + j, 4), None)

        return carry

    lax.fori_loop(0, STEPS, step, 0)
    loss_ref[...] = jnp.sum(loss_sum[...].T, axis=0, keepdims=True)
    backward_rows(image_ref, image_mag, image_sum, image_out)

    def last(r, carry):
        @pl.when(r > 0)
        def _():
            def arrived(k, c):
                at = pl.ds(pl.multiple_of(k * part, part), part)
                pltpu.make_async_remote_copy(
                    src_ref=own.at[at], dst_ref=held.at[FAR + r, at],
                    send_sem=far_send.at[k], recv_sem=pass_recv.at[r - 1, k],
                    device_id=far, device_id_type=MESH,
                ).wait_recv()
                return c
            lax.fori_loop(PIECES, STEPS, arrived, 0)
            tile_copy(0, OWN, FAR + r, after).wait_recv()

        text_side(FAR + r, g, None)
        return carry

    lax.fori_loop(0, 4, last, 0)
    backward_rows(text_ref, text_mag, text_sum, text_out)

    for i, (device, slot) in enumerate(targets):
        tile_copy(i, OWN, slot, device).wait_send()
        slot_copy(i, own, slot, device).wait_send()
    tile_copy(6, OWN, FAR, far).wait_send()
    tile_copy(7, source, place, twin).wait_send()
    slot_copy(6, held.at[source], place, twin).wait_send()
    for dy in (1, 2, 3):
        tile_copy(7 + dy, FAR, FAR + 4 - dy, near(dy)).wait_send()

    def sent(j, carry):
        for dy in (1, 2, 3):
            pass_copy(dy, j).wait_send()
        return carry

    lax.fori_loop(0, STEPS, sent, 0)


def on_device(image_emb, text_emb, loop_mask, neg_list):
    rows, width = image_emb.shape
    vmem = pl.BlockSpec(memory_space=pltpu.VMEM)
    smem = pl.BlockSpec(memory_space=pltpu.SMEM)
    losses, image_grad, text_grad = pl.pallas_call(
        kernel,
        out_shape=(
            jax.ShapeDtypeStruct((1, rows), jnp.float32),
            jax.ShapeDtypeStruct((rows, width), jnp.bfloat16),
            jax.ShapeDtypeStruct((rows, width), jnp.bfloat16),
        ),
        in_specs=[vmem, vmem, smem, smem],
        out_specs=(vmem, vmem, vmem),
        scratch_shapes=[
            pltpu.VMEM((2 * rows, width), jnp.bfloat16),
            pltpu.VMEM((12, 2 * rows, width), jnp.bfloat16),
            pltpu.VMEM((12, 8, 128), jnp.float32),
            pltpu.VMEM((rows, 1), jnp.float32),
            pltpu.VMEM((rows, 1), jnp.float32),
            pltpu.VMEM((rows, width), jnp.float32),
            pltpu.VMEM((rows, width), jnp.float32),
            pltpu.VMEM((rows, rows), jnp.float32),
            pltpu.SemaphoreType.DMA((STEPS,)),
            pltpu.SemaphoreType.DMA((STEPS,)),
            pltpu.SemaphoreType.DMA((7,)),
            pltpu.SemaphoreType.DMA((8,)),
            pltpu.SemaphoreType.DMA((11,)),
            pltpu.SemaphoreType.DMA((12,)),
            pltpu.SemaphoreType.DMA((3, STEPS)),
            pltpu.SemaphoreType.DMA((3, STEPS)),
        ],
        compiler_params=pltpu.CompilerParams(
            collective_id=0, has_side_effects=True, vmem_limit_bytes=32 * 2**20
        ),
        name="pair_blocks",
    )(image_emb, text_emb, loop_mask, neg_list)
    return losses.reshape(rows), image_grad, text_grad


def solution(mesh):
    placed = (
        P(("blk", "grp"), None),
        P(("blk", "grp"), None),
        P(("blk", "grp"), None),
        P(("blk", "grp"), None),
    )
    return jax.shard_map(
        on_device,
        mesh=mesh,
        in_specs=placed,
        out_specs=(P(("blk", "grp")), P(("blk", "grp"), None), P(("blk", "grp"), None)),
        check_vma=False,
    )
```

```python
import jax
import jax.numpy as jnp
from jax import lax
from jax.experimental import pallas as pl
from jax.experimental.pallas import tpu as pltpu
from jax.sharding import PartitionSpec as P

MESH = pl.DeviceIdType.MESH

epsilon = 1e-06
logit_scale = 16.0
logit_bias = -2.0

PIECES = 4
LAG = 1
OWN = 4
FAR = 8


def normalize_rows(emb_ref, mag_ref, unit_ref, first):
    rows = emb_ref.shape[0]

    def some(i, carry):
        at = pl.ds(pl.multiple_of(i * 16, 16), 16)
        values = emb_ref[at, :].astype(jnp.float32)
        magnitude = jnp.sqrt(jnp.sum(values * values, axis=-1, keepdims=True) + epsilon)
        mag_ref[at, :] = magnitude
        unit = (values / magnitude).astype(jnp.bfloat16)
        unit_ref[pl.ds(pl.multiple_of(first + i * 16, 16), 16), :] = unit
        return carry

    lax.fori_loop(0, rows // 16, some, 0)


def backward_rows(emb_ref, mag_ref, sum_ref, more_ref, out_ref, first, count):
    def some(i, carry):
        at = pl.ds(pl.multiple_of(first + i * 16, 16), 16)
        magnitude = mag_ref[at, :]
        full = emb_ref[at, :].astype(jnp.float32) / magnitude
        grad = sum_ref[at, :]
        if more_ref is not None:
            grad = grad + more_ref[at, :].astype(jnp.float32)
        grad = logit_scale * grad
        along = jnp.sum(full * grad, axis=-1, keepdims=True)
        out_ref[at, :] = ((grad - full * along) / magnitude).astype(jnp.bfloat16)
        return carry

    lax.fori_loop(0, count // 16, some, 0)


def kernel(
    image_hbm, text_hbm, mask_ref, neg_ref,
    loss_ref, image_out, text_out,
    image_ref, text_ref, own, held, tiles, image_mag, text_mag, image_sum, text_sum, loss_sum,
    far_weight, sent_back, got_back,
    load_sem, far_send, far_recv, slot_send, slot_recv, tile_send, tile_recv, pass_send, pass_recv,
    back_send, back_recv,
):
    rows = image_ref.shape[0]
    part = rows // PIECES
    p = lax.axis_index("blk")
    g = lax.axis_index("grp")
    n = lax.axis_size("blk")
    half, y = g // 4, lax.rem(g, 4)
    core = lax.rem(p, 2)
    low, high = p < 2, p >= n - 2
    closing = low | high

    def near(dy):
        return (p, half * 4 + lax.rem(y + dy, 4))

    other_half = lax.rem(g + 4, 8)
    far = (p, other_half)
    next_p, last_p = lax.rem(p + 2, n), lax.rem(p + n - 2, n)
    after, before = (next_p, g), (last_p, g)
    twin = (p + 1 - 2 * core, g)
    partners = [far, after, before, twin, near(1), near(2), near(3)]

    barrier = pltpu.get_barrier_semaphore()
    for device in partners:
        pl.semaphore_signal(barrier, inc=1, device_id=device, device_id_type=MESH)

    load_text = pltpu.make_async_copy(text_hbm, text_ref, load_sem.at[0])
    load_image = pltpu.make_async_copy(image_hbm, image_ref, load_sem.at[1])
    load_text.start()
    load_image.start()

    lane = lax.broadcasted_iota(jnp.int32, (8, 128), 1)
    mine = (lane == neg_ref[0, 0]) | (lane == neg_ref[0, 1]) | (lane == g)
    tile = jnp.where(mine, 1.0, 0.0)
    for k in range(4):
        tile = jnp.where(lane == 8 + k, mask_ref[0, k].astype(jnp.float32), tile)
    tiles[OWN] = tile
    load_text.wait()
    normalize_rows(text_ref, text_mag, own, 0)

    def slot_rows(slot):
        return pl.ds(pl.multiple_of(slot * (2 * rows), 2 * rows), 2 * rows)

    def piece(j, source):
        return pl.ds(pl.multiple_of(FAR * 2 * rows + j * (4 * part) + source * part, part), part)

    def far_copy(j):
        at = pl.ds(pl.multiple_of(j * part, part), part)
        return pltpu.make_async_remote_copy(
            src_ref=own.at[at], dst_ref=held.at[piece(j, 0)],
            send_sem=far_send.at[j], recv_sem=far_recv.at[j],
            device_id=far, device_id_type=MESH,
        )

    def slot_copy(i, src, slot, device):
        return pltpu.make_async_remote_copy(
            src_ref=src, dst_ref=held.at[slot_rows(slot)],
            send_sem=slot_send.at[i], recv_sem=slot_recv.at[slot],
            device_id=device, device_id_type=MESH,
        )

    def tile_copy(i, src_slot, slot, device):
        return pltpu.make_async_remote_copy(
            src_ref=tiles.at[src_slot], dst_ref=tiles.at[slot],
            send_sem=tile_send.at[i], recv_sem=tile_recv.at[slot],
            device_id=device, device_id_type=MESH,
        )

    def pass_copy(dy, j):
        return pltpu.make_async_remote_copy(
            src_ref=held.at[piece(j, 0)], dst_ref=held.at[piece(j, 4 - dy)],
            send_sem=pass_send.at[dy - 1, j], recv_sem=pass_recv.at[3 - dy, j],
            device_id=near(dy), device_id_type=MESH,
        )

    def back_copy(j):
        at = pl.ds(pl.multiple_of(j * part, part), part)
        return pltpu.make_async_remote_copy(
            src_ref=sent_back.at[at], dst_ref=got_back.at[at],
            send_sem=back_send.at[j], recv_sem=back_recv.at[j],
            device_id=far, device_id_type=MESH,
        )

    pl.semaphore_wait(barrier, len(partners))

    def send_far(j, carry):
        far_copy(j).start()
        return carry

    lax.fori_loop(0, PIECES, send_far, 0)
    load_image.wait()
    normalize_rows(image_ref, image_mag, own, rows)

    targets = [(after, 0), (before, 3), (twin, 1 + core)] + [(near(dy), OWN + 4 - dy) for dy in (1, 2, 3)]
    for i, (device, slot) in enumerate(targets):
        tile_copy(i, OWN, slot, device).start()
    for i in (3, 4, 5, 2, 0, 1):
        device, slot = targets[i]
        slot_copy(i, own, slot, device).start()

    held[slot_rows(OWN), :] = own[...]
    image_sum[...] = jnp.zeros_like(image_sum)
    text_sum[...] = jnp.zeros_like(text_sum)
    loss_sum[...] = jnp.zeros_like(loss_sum)

    source, place = 3 - 3 * core, 2 - core
    late = (low & (core == 1)) | (high & (core == 0))

    row = lax.broadcasted_iota(jnp.int32, (rows, rows), 0)
    column = lax.broadcasted_iota(jnp.int32, (rows, rows), 1)
    eye = jnp.where(row == column, 1.0, 0.0)
    first_lane = lax.broadcasted_iota(jnp.int32, (1, 128), 1)

    def weight(slot, index):
        picked = jnp.where(first_lane == index, tiles[slot, 0:1, :], 0.0)
        return jnp.sum(picked, axis=1, keepdims=True)

    def scores_of(own_block, other):
        return logit_scale * lax.dot_general(
            own_block, other, (((1,), (1,)), ((), ())), preferred_element_type=jnp.float32
        ) + logit_bias

    def sigmoid_of(scores):
        small = jnp.exp(-jnp.abs(scores))
        return jnp.where(scores >= 0.0, 1.0, small) / (1.0 + small)

    def image_side(other, w, diagonal):
        scores = scores_of(own[pl.ds(rows, rows), :], other)
        small = jnp.exp(-jnp.abs(scores))
        loss = jnp.maximum(scores, 0.0) + jnp.log1p(small)
        grad = jnp.where(scores >= 0.0, 1.0, small) / (1.0 + small)
        if diagonal is not None:
            loss = loss - diagonal * scores
            grad = grad - diagonal
        loss_sum[...] += w * loss
        image_sum[...] += jnp.dot(
            (w * grad).astype(jnp.bfloat16), other, preferred_element_type=jnp.float32
        )

    def text_side(other, w, diagonal):
        scores = scores_of(own[pl.ds(0, rows), :], other)
        text_sum[...] += jnp.dot(
            (w * (sigmoid_of(scores) - diagonal)).astype(jnp.bfloat16), other, preferred_element_type=jnp.float32
        )

    def unit(slot):
        in_loop = slot < 4
        group_index = half * 4 + lax.rem(y + slot, 4)
        diagonal = jnp.where(slot == OWN, 1.0, 0.0) * eye
        first = pl.multiple_of(slot * (2 * rows), 2 * rows)
        w = weight(OWN, jnp.where(in_loop, 8 + slot, group_index))
        image_side(held[pl.ds(first, rows), :], w, diagonal)
        w = weight(slot, jnp.where(in_loop, 11 - slot, g))
        text_side(held[pl.ds(first + rows, rows), :], w, diagonal)

    def far_weights():
        w = jnp.zeros((1, 128), jnp.float32)
        for r in range(4):
            w = jnp.where(first_lane // part == r, weight(OWN, (1 - half) * 4 + lax.rem(y + r, 4)), w)
            far_weight[r] = jnp.broadcast_to(weight(OWN + r, other_half), (8, 128))
        far_weight[4] = jnp.broadcast_to(w, (8, 128))

    def far_piece(k):
        first = pl.multiple_of(FAR * 2 * rows + k * (4 * part), 4 * part)
        return held[pl.ds(first, 4 * part), :]

    def arrived(k):
        for dy in (1, 2, 3):
            pass_copy(dy, k).wait_recv()

    def relay():
        slot_copy(6, held.at[slot_rows(source)], source, twin).wait_recv()
        slot_copy(6, held.at[slot_rows(source)], place, twin).start()
        tile_copy(6, source, source, twin).wait_recv()
        tile_copy(6, source, place, twin).start()

    def units(slot, carry):
        @pl.when((slot != OWN) & (slot != source))
        def _():
            slot_copy(0, own, slot, after).wait_recv()
            tile_copy(0, OWN, slot, after).wait_recv()

        unit(slot)
        return carry

    @pl.when(jnp.logical_not(late))
    def _():
        relay()

    lax.fori_loop(OWN, OWN + 4, units, 0)
    far_weights()

    @pl.when(jnp.logical_not(closing))
    def _():
        lax.fori_loop(0, 4, units, 0)

    def step(j, carry):
        far_copy(j).wait_recv()
        for dy in (1, 2, 3):
            pass_copy(dy, j).start()

        text_piece = held[piece(j, 0), :]
        total = jnp.zeros((part, image_ref.shape[1]), jnp.float32)
        for r in range(4):
            images = held[pl.ds((OWN + r) * 2 * rows + rows, rows), :]
            scores = scores_of(text_piece, images)
            grad = far_weight[r, 0:1, :] * sigmoid_of(scores)
            total += jnp.dot(grad.astype(jnp.bfloat16), images, preferred_element_type=jnp.float32)
        sent_back[pl.ds(pl.multiple_of(j * part, part), part), :] = total.astype(jnp.bfloat16)
        back_copy(j).start()

        @pl.when(j >= LAG)
        def _():
            far_image(j - LAG)

        return carry

    def far_image(k):
        arrived(k)
        image_side(far_piece(k), far_weight[4, 0:1, :], None)

    lax.fori_loop(0, PIECES, step, 0)

    @pl.when(closing)
    def _():
        @pl.when(late)
        def _():
            relay()

        lax.fori_loop(0, 4, units, 0)

    for k in range(PIECES - LAG, PIECES):
        far_image(k)
    loss_ref[...] = jnp.sum(loss_sum[...].T, axis=0, keepdims=True)
    backward_rows(image_ref, image_mag, image_sum, None, image_out, 0, rows)

    def finish(j, carry):
        back_copy(j).wait_recv()
        backward_rows(text_ref, text_mag, text_sum, got_back, text_out, j * part, part)
        return carry

    lax.fori_loop(0, PIECES, finish, 0)

    for i, (device, slot) in enumerate(targets):
        tile_copy(i, OWN, slot, device).wait_send()
        slot_copy(i, own, slot, device).wait_send()
    tile_copy(6, source, place, twin).wait_send()
    slot_copy(6, held.at[slot_rows(source)], place, twin).wait_send()

    def sent(j, carry):
        for dy in (1, 2, 3):
            pass_copy(dy, j).wait_send()
        far_copy(j).wait_send()
        back_copy(j).wait_send()
        return carry

    lax.fori_loop(0, PIECES, sent, 0)


def on_device(image_emb, text_emb, loop_mask, neg_list):
    rows, width = image_emb.shape
    vmem = pl.BlockSpec(memory_space=pltpu.VMEM)
    hbm = pl.BlockSpec(memory_space=pl.ANY)
    smem = pl.BlockSpec(memory_space=pltpu.SMEM)
    losses, image_grad, text_grad = pl.pallas_call(
        kernel,
        out_shape=(
            jax.ShapeDtypeStruct((1, rows), jnp.float32),
            jax.ShapeDtypeStruct((rows, width), jnp.bfloat16),
            jax.ShapeDtypeStruct((rows, width), jnp.bfloat16),
        ),
        in_specs=[hbm, hbm, smem, smem],
        out_specs=(vmem, vmem, vmem),
        scratch_shapes=[
            pltpu.VMEM((rows, width), jnp.bfloat16),
            pltpu.VMEM((rows, width), jnp.bfloat16),
            pltpu.VMEM((2 * rows, width), jnp.bfloat16),
            pltpu.VMEM((FAR * 2 * rows + 4 * rows, width), jnp.bfloat16),
            pltpu.VMEM((8, 8, 128), jnp.float32),
            pltpu.VMEM((rows, 1), jnp.float32),
            pltpu.VMEM((rows, 1), jnp.float32),
            pltpu.VMEM((rows, width), jnp.float32),
            pltpu.VMEM((rows, width), jnp.float32),
            pltpu.VMEM((rows, rows), jnp.float32),
            pltpu.VMEM((5, 8, 128), jnp.float32),
            pltpu.VMEM((rows, width), jnp.bfloat16),
            pltpu.VMEM((rows, width), jnp.bfloat16),
            pltpu.SemaphoreType.DMA((2,)),
            pltpu.SemaphoreType.DMA((PIECES,)),
            pltpu.SemaphoreType.DMA((PIECES,)),
            pltpu.SemaphoreType.DMA((7,)),
            pltpu.SemaphoreType.DMA((8,)),
            pltpu.SemaphoreType.DMA((7,)),
            pltpu.SemaphoreType.DMA((8,)),
            pltpu.SemaphoreType.DMA((3, PIECES)),
            pltpu.SemaphoreType.DMA((3, PIECES)),
            pltpu.SemaphoreType.DMA((PIECES,)),
            pltpu.SemaphoreType.DMA((PIECES,)),
        ],
        compiler_params=pltpu.CompilerParams(
            collective_id=0, has_side_effects=True, vmem_limit_bytes=32 * 2**20
        ),
        name="pair_blocks",
    )(image_emb, text_emb, loop_mask, neg_list)
    return losses.reshape(rows), image_grad, text_grad


def solution(mesh):
    placed = (
        P(("blk", "grp"), None),
        P(("blk", "grp"), None),
        P(("blk", "grp"), None),
        P(("blk", "grp"), None),
    )
    return jax.shard_map(
        on_device,
        mesh=mesh,
        in_specs=placed,
        out_specs=(P(("blk", "grp")), P(("blk", "grp"), None), P(("blk", "grp"), None)),
        check_vma=False,
    )
```

```python
import jax
import jax.numpy as jnp
from jax import lax
from jax.experimental import pallas as pl
from jax.experimental.pallas import tpu as pltpu
from jax.sharding import PartitionSpec as P

MESH = pl.DeviceIdType.MESH

epsilon = 1e-06
logit_scale = 16.0
logit_bias = -2.0

PIECES = 4
BITS = 2 * PIECES
LAG = 1
OWN = 4
FAR = 8


def normalize_rows(emb_ref, mag_ref, unit_ref, first):
    rows = emb_ref.shape[0]

    def some(i, carry):
        at = pl.ds(pl.multiple_of(i * 16, 16), 16)
        values = emb_ref[at, :].astype(jnp.float32)
        magnitude = jnp.sqrt(jnp.sum(values * values, axis=-1, keepdims=True) + epsilon)
        mag_ref[at, :] = magnitude
        unit = (values / magnitude).astype(jnp.bfloat16)
        unit_ref[pl.ds(pl.multiple_of(first + i * 16, 16), 16), :] = unit
        return carry

    lax.fori_loop(0, rows // 16, some, 0, unroll=4)


def backward_rows(emb_ref, mag_ref, sum_ref, more_ref, out_ref, first, count):
    def some(i, carry):
        at = pl.ds(pl.multiple_of(first + i * 16, 16), 16)
        magnitude = mag_ref[at, :]
        full = emb_ref[at, :].astype(jnp.float32) / magnitude
        grad = sum_ref[at, :]
        if more_ref is not None:
            grad = grad + more_ref[at, :].astype(jnp.float32)
        grad = logit_scale * grad
        along = jnp.sum(full * grad, axis=-1, keepdims=True)
        out_ref[at, :] = ((grad - full * along) / magnitude).astype(jnp.bfloat16)
        return carry

    lax.fori_loop(0, count // 16, some, 0, unroll=2)


def kernel(
    image_hbm, text_hbm, mask_hbm, neg_hbm,
    loss_ref, image_out, text_out,
    image_ref, text_ref, mask_ref, neg_ref, own, held, tiles, image_mag, text_mag, image_sum, text_sum, loss_sum,
    far_weight, sent_back, got_back, detour,
    load_sem, far_send, far_recv, slot_send, slot_recv, tile_send, tile_recv, pass_send, pass_recv,
    back_send, back_recv, detour_send, detour_recv,
):
    rows = image_ref.shape[0]
    part = rows // PIECES
    p = lax.axis_index("blk")
    g = lax.axis_index("grp")
    n = lax.axis_size("blk")
    half, y = g // 4, lax.rem(g, 4)
    core = lax.rem(p, 2)
    x = lax.rem(p // 2, 4)
    low, high = x == 0, x == 3
    turning = low | high
    beside = p + 2 - 4 * lax.rem(x, 2)

    def near(dy):
        return (p, half * 4 + lax.rem(y + dy, 4))

    other_half = lax.rem(g + 4, 8)
    far = (p, other_half)
    next_p, last_p = lax.rem(p + 2, n), lax.rem(p + n - 2, n)
    after, before = (next_p, g), (last_p, g)
    twin = (p + 1 - 2 * core, g)
    partners = [far, (beside, other_half), after, before, twin, near(1), near(2), near(3)]

    barrier = pltpu.get_barrier_semaphore()
    for device in partners:
        pl.semaphore_signal(barrier, inc=1, device_id=device, device_id_type=MESH)

    load_text = pltpu.make_async_copy(text_hbm, text_ref, load_sem.at[0])
    load_image = pltpu.make_async_copy(image_hbm, image_ref, load_sem.at[1])
    load_mask = pltpu.make_async_copy(mask_hbm, mask_ref, load_sem.at[2])
    load_neg = pltpu.make_async_copy(neg_hbm, neg_ref, load_sem.at[3])
    loads = [load_text, load_image, load_mask, load_neg]
    for load in loads:
        load.start()
    load_text.wait()
    normalize_rows(text_ref, text_mag, own, 0)
    load_mask.wait()
    load_neg.wait()
    lane = lax.broadcasted_iota(jnp.int32, (8, 128), 1)
    mine = (lane == neg_ref[0, 0]) | (lane == neg_ref[0, 1]) | (lane == g)
    tile = jnp.where(mine, 1.0, 0.0)
    for k in range(4):
        tile = jnp.where(lane == 8 + k, mask_ref[0, k].astype(jnp.float32), tile)
    tiles[OWN] = tile

    def slot_rows(slot):
        return pl.ds(pl.multiple_of(slot * (2 * rows), 2 * rows), 2 * rows)

    def piece(j, source):
        return pl.ds(pl.multiple_of(FAR * 2 * rows + j * (4 * part) + source * part, part), part)

    bit = part // 2

    def landing(i):
        first = FAR * 2 * rows + i // 2 * (4 * part) + lax.rem(i, 2) * bit
        return pl.ds(pl.multiple_of(first, bit), bit)

    def far_copy(i):
        return pltpu.make_async_remote_copy(
            src_ref=own.at[pl.ds(pl.multiple_of(i * bit, bit), bit)], dst_ref=held.at[landing(i)],
            send_sem=far_send.at[i], recv_sem=far_recv.at[i],
            device_id=far, device_id_type=MESH,
        )

    out_copy = pltpu.make_async_remote_copy(
        src_ref=own.at[pl.ds((BITS - 1) * bit, bit)], dst_ref=detour,
        send_sem=far_send.at[BITS - 1], recv_sem=detour_recv,
        device_id=(beside, other_half), device_id_type=MESH,
    )
    in_copy = pltpu.make_async_remote_copy(
        src_ref=detour, dst_ref=held.at[landing(BITS - 1)],
        send_sem=detour_send, recv_sem=far_recv.at[BITS - 1],
        device_id=(beside, g), device_id_type=MESH,
    )

    def slot_copy(i, src, slot, device):
        return pltpu.make_async_remote_copy(
            src_ref=src, dst_ref=held.at[slot_rows(slot)],
            send_sem=slot_send.at[i], recv_sem=slot_recv.at[slot],
            device_id=device, device_id_type=MESH,
        )

    def tile_copy(i, src_slot, slot, device):
        return pltpu.make_async_remote_copy(
            src_ref=tiles.at[src_slot], dst_ref=tiles.at[slot],
            send_sem=tile_send.at[i], recv_sem=tile_recv.at[slot],
            device_id=device, device_id_type=MESH,
        )

    def pass_copy(dy, j):
        return pltpu.make_async_remote_copy(
            src_ref=held.at[piece(j, 0)], dst_ref=held.at[piece(j, 4 - dy)],
            send_sem=pass_send.at[dy - 1, j], recv_sem=pass_recv.at[3 - dy, j],
            device_id=near(dy), device_id_type=MESH,
        )

    def back_copy(j):
        at = pl.ds(pl.multiple_of(j * part, part), part)
        return pltpu.make_async_remote_copy(
            src_ref=sent_back.at[at], dst_ref=got_back.at[at],
            send_sem=back_send.at[j], recv_sem=back_recv.at[j],
            device_id=far, device_id_type=MESH,
        )

    pl.semaphore_wait(barrier, len(partners))

    def send_far(j, carry):
        far_copy(j).start()
        return carry


    @pl.when(turning)
    def _():
        out_copy.start()

    lax.fori_loop(0, BITS - 1, send_far, 0)

    @pl.when(jnp.logical_not(turning))
    def _():
        far_copy(BITS - 1).start()

    load_image.wait()
    normalize_rows(image_ref, image_mag, own, rows)
    targets = [(after, 0), (before, 3), (twin, 1 + core)] + [(near(dy), OWN + 4 - dy) for dy in (1, 2, 3)]
    for i, (device, slot) in enumerate(targets):
        tile_copy(i, OWN, slot, device).start()
    for i in (3, 4, 5, 2, 0, 1):
        device, slot = targets[i]
        slot_copy(i, own, slot, device).start()

    held[slot_rows(OWN), :] = own[...]
    image_sum[...] = jnp.zeros_like(image_sum)
    text_sum[...] = jnp.zeros_like(text_sum)
    loss_sum[...] = jnp.zeros_like(loss_sum)

    source, place = 3 - 3 * core, 2 - core
    late = (low & (core == 1)) | (high & (core == 0))

    row = lax.broadcasted_iota(jnp.int32, (rows, rows), 0)
    column = lax.broadcasted_iota(jnp.int32, (rows, rows), 1)
    eye = jnp.where(row == column, 1.0, 0.0)
    first_lane = lax.broadcasted_iota(jnp.int32, (1, 128), 1)

    def weight(slot, index):
        picked = jnp.where(first_lane == index, tiles[slot, 0:1, :], 0.0)
        return jnp.sum(picked, axis=1, keepdims=True)

    def scores_of(own_block, other):
        return logit_scale * lax.dot_general(
            own_block, other, (((1,), (1,)), ((), ())), preferred_element_type=jnp.float32
        ) + logit_bias

    def sigmoid_of(scores):
        small = jnp.exp(-jnp.abs(scores))
        return jnp.where(scores >= 0.0, 1.0, small) / (1.0 + small)

    def image_side(other, w, diagonal):
        scores = scores_of(own[pl.ds(rows, rows), :], other)
        small = jnp.exp(-jnp.abs(scores))
        loss = jnp.maximum(scores, 0.0) + jnp.log1p(small)
        grad = jnp.where(scores >= 0.0, 1.0, small) / (1.0 + small)
        if diagonal is not None:
            loss = loss - diagonal * scores
            grad = grad - diagonal
        loss_sum[...] += w * loss
        image_sum[...] += jnp.dot(
            (w * grad).astype(jnp.bfloat16), other, preferred_element_type=jnp.float32
        )

    def text_side(other, w, diagonal):
        scores = scores_of(own[pl.ds(0, rows), :], other)
        text_sum[...] += jnp.dot(
            (w * (sigmoid_of(scores) - diagonal)).astype(jnp.bfloat16), other, preferred_element_type=jnp.float32
        )

    def unit(slot):
        in_loop = slot < 4
        group_index = half * 4 + lax.rem(y + slot, 4)
        diagonal = jnp.where(slot == OWN, 1.0, 0.0) * eye
        first = pl.multiple_of(slot * (2 * rows), 2 * rows)
        w = weight(OWN, jnp.where(in_loop, 8 + slot, group_index))
        image_side(held[pl.ds(first, rows), :], w, diagonal)
        w = weight(slot, jnp.where(in_loop, 11 - slot, g))
        text_side(held[pl.ds(first + rows, rows), :], w, diagonal)

    def far_weights():
        w = jnp.zeros((1, 128), jnp.float32)
        for r in range(4):
            w = jnp.where(first_lane // part == r, weight(OWN, (1 - half) * 4 + lax.rem(y + r, 4)), w)
            far_weight[r] = jnp.broadcast_to(weight(OWN + r, other_half), (8, 128))
        far_weight[4] = jnp.broadcast_to(w, (8, 128))

    def far_piece(k):
        first = pl.multiple_of(FAR * 2 * rows + k * (4 * part), 4 * part)
        return held[pl.ds(first, 4 * part), :]

    def arrived(k):
        for dy in (1, 2, 3):
            pass_copy(dy, k).wait_recv()

    def relay():
        slot_copy(6, held.at[slot_rows(source)], source, twin).wait_recv()
        slot_copy(6, held.at[slot_rows(source)], place, twin).start()
        tile_copy(6, source, source, twin).wait_recv()
        tile_copy(6, source, place, twin).start()

    def units(slot, carry):
        @pl.when((slot != OWN) & (slot != source))
        def _():
            slot_copy(0, own, slot, after).wait_recv()
            tile_copy(0, OWN, slot, after).wait_recv()

        unit(slot)
        return carry

    @pl.when(jnp.logical_not(late))
    def _():
        relay()

    lax.fori_loop(OWN, OWN + 4, units, 0)
    far_weights()

    @pl.when(jnp.logical_not(turning))
    def _():
        lax.fori_loop(0, 4, units, 0)

    def step(j, carry):
        @pl.when((j == PIECES - 2) & jnp.logical_not(turning))
        def _():
            out_copy.wait_recv()
            in_copy.start()

        far_copy(2 * j).wait_recv()
        far_copy(2 * j + 1).wait_recv()
        for dy in (1, 2, 3):
            pass_copy(dy, j).start()

        text_piece = held[piece(j, 0), :]
        total = jnp.zeros((part, image_ref.shape[1]), jnp.float32)
        for r in range(4):
            images = held[pl.ds((OWN + r) * 2 * rows + rows, rows), :]
            scores = scores_of(text_piece, images)
            grad = far_weight[r, 0:1, :] * sigmoid_of(scores)
            total += jnp.dot(grad.astype(jnp.bfloat16), images, preferred_element_type=jnp.float32)
        sent_back[pl.ds(pl.multiple_of(j * part, part), part), :] = total.astype(jnp.bfloat16)
        back_copy(j).start()

        @pl.when(j >= LAG)
        def _():
            far_image(j - LAG)

        return carry

    def far_image(k):
        arrived(k)
        image_side(far_piece(k), far_weight[4, 0:1, :], None)

    lax.fori_loop(0, PIECES, step, 0)

    @pl.when(turning)
    def _():
        @pl.when(late)
        def _():
            relay()

        lax.fori_loop(0, 4, units, 0)

    for k in range(PIECES - LAG, PIECES):
        far_image(k)
    loss_ref[...] = jnp.sum(loss_sum[...].T, axis=0, keepdims=True)
    backward_rows(image_ref, image_mag, image_sum, None, image_out, 0, rows)

    def finish(j, carry):
        back_copy(j).wait_recv()
        backward_rows(text_ref, text_mag, text_sum, got_back, text_out, j * part, part)
        return carry

    lax.fori_loop(0, PIECES, finish, 0)

    for i, (device, slot) in enumerate(targets):
        tile_copy(i, OWN, slot, device).wait_send()
        slot_copy(i, own, slot, device).wait_send()
    tile_copy(6, source, place, twin).wait_send()
    slot_copy(6, held.at[slot_rows(source)], place, twin).wait_send()

    def sent(j, carry):
        for dy in (1, 2, 3):
            pass_copy(dy, j).wait_send()
        far_copy(2 * j).wait_send()
        far_copy(2 * j + 1).wait_send()
        back_copy(j).wait_send()
        return carry

    lax.fori_loop(0, PIECES, sent, 0)

    @pl.when(jnp.logical_not(turning))
    def _():
        in_copy.wait_send()


def on_device(image_emb, text_emb, loop_mask, neg_list):
    rows, width = image_emb.shape
    vmem = pl.BlockSpec(memory_space=pltpu.VMEM)
    hbm = pl.BlockSpec(memory_space=pltpu.HBM)
    losses, image_grad, text_grad = pl.pallas_call(
        kernel,
        out_shape=(
            jax.ShapeDtypeStruct((1, rows), jnp.float32),
            jax.ShapeDtypeStruct((rows, width), jnp.bfloat16),
            jax.ShapeDtypeStruct((rows, width), jnp.bfloat16),
        ),
        in_specs=[hbm] * 4,
        out_specs=(vmem, vmem, vmem),
        scratch_shapes=[
            pltpu.VMEM((rows, width), jnp.bfloat16),
            pltpu.VMEM((rows, width), jnp.bfloat16),
            pltpu.SMEM(loop_mask.shape, jnp.int32),
            pltpu.SMEM(neg_list.shape, jnp.int32),
            pltpu.VMEM((2 * rows, width), jnp.bfloat16),
            pltpu.VMEM((FAR * 2 * rows + 4 * rows, width), jnp.bfloat16),
            pltpu.VMEM((8, 8, 128), jnp.float32),
            pltpu.VMEM((rows, 1), jnp.float32),
            pltpu.VMEM((rows, 1), jnp.float32),
            pltpu.VMEM((rows, width), jnp.float32),
            pltpu.VMEM((rows, width), jnp.float32),
            pltpu.VMEM((rows, rows), jnp.float32),
            pltpu.VMEM((5, 8, 128), jnp.float32),
            pltpu.VMEM((rows, width), jnp.bfloat16),
            pltpu.VMEM((rows, width), jnp.bfloat16),
            pltpu.VMEM((rows // BITS, width), jnp.bfloat16),
            pltpu.SemaphoreType.DMA((4,)),
            pltpu.SemaphoreType.DMA((BITS,)),
            pltpu.SemaphoreType.DMA((BITS,)),
            pltpu.SemaphoreType.DMA((7,)),
            pltpu.SemaphoreType.DMA((8,)),
            pltpu.SemaphoreType.DMA((7,)),
            pltpu.SemaphoreType.DMA((8,)),
            pltpu.SemaphoreType.DMA((3, PIECES)),
            pltpu.SemaphoreType.DMA((3, PIECES)),
            pltpu.SemaphoreType.DMA((PIECES,)),
            pltpu.SemaphoreType.DMA((PIECES,)),
            pltpu.SemaphoreType.DMA,
            pltpu.SemaphoreType.DMA,
        ],
        compiler_params=pltpu.CompilerParams(
            collective_id=0, has_side_effects=True, vmem_limit_bytes=60 * 2**20
        ),
        name="pair_blocks",
    )(image_emb, text_emb, loop_mask, neg_list)
    return losses.reshape(rows), image_grad, text_grad


def solution(mesh):
    placed = (
        P(("blk", "grp"), None),
        P(("blk", "grp"), None),
        P(("blk", "grp"), None),
        P(("blk", "grp"), None),
    )
    return jax.shard_map(
        on_device,
        mesh=mesh,
        in_specs=placed,
        out_specs=(P(("blk", "grp")), P(("blk", "grp"), None), P(("blk", "grp"), None)),
        check_vma=False,
    )
```

```python
import jax
import jax.numpy as jnp
from jax import lax
from jax.experimental import pallas as pl
from jax.experimental.pallas import tpu as pltpu
from jax.sharding import PartitionSpec as P

MESH = pl.DeviceIdType.MESH

epsilon = 1e-06
logit_scale = 16.0
logit_bias = -2.0

PIECES = 4
BITS = 2 * PIECES
LAG = 1
OWN = 4
FAR = 8


def normalize_rows(emb_ref, mag_ref, unit_ref, first):
    rows = emb_ref.shape[0]

    def some(i, carry):
        at = pl.ds(pl.multiple_of(i * 16, 16), 16)
        values = emb_ref[at, :].astype(jnp.float32)
        magnitude = jnp.sqrt(jnp.sum(values * values, axis=-1, keepdims=True) + epsilon)
        mag_ref[at, :] = magnitude
        unit = (values / magnitude).astype(jnp.bfloat16)
        unit_ref[pl.ds(pl.multiple_of(first + i * 16, 16), 16), :] = unit
        return carry

    lax.fori_loop(0, rows // 16, some, 0, unroll=4)


def backward_rows(emb_ref, mag_ref, sum_ref, more_ref, out_ref, first, count):
    def some(i, carry):
        at = pl.ds(pl.multiple_of(first + i * 16, 16), 16)
        magnitude = mag_ref[at, :]
        full = emb_ref[at, :].astype(jnp.float32) / magnitude
        grad = sum_ref[at, :]
        if more_ref is not None:
            grad = grad + more_ref[at, :].astype(jnp.float32)
        grad = logit_scale * grad
        along = jnp.sum(full * grad, axis=-1, keepdims=True)
        out_ref[at, :] = ((grad - full * along) / magnitude).astype(jnp.bfloat16)
        return carry

    lax.fori_loop(0, count // 16, some, 0, unroll=2)


def kernel(
    image_hbm, text_hbm, mask_hbm, neg_hbm,
    loss_ref, image_out, text_out,
    image_ref, text_ref, mask_ref, neg_ref, own, held, tiles, image_mag, text_mag, image_sum, text_sum, loss_sum,
    far_weight, sent_back, got_back,
    load_sem, far_send, far_recv, slot_send, slot_recv, tile_send, tile_recv, pass_send, pass_recv,
    back_send, back_recv, edge_send, edge_recv, around_send, around_recv,
):
    rows = image_ref.shape[0]
    part = rows // PIECES
    p = lax.axis_index("blk")
    g = lax.axis_index("grp")
    n = lax.axis_size("blk")
    half, y = g // 4, lax.rem(g, 4)
    core = lax.rem(p, 2)
    x = lax.rem(p // 2, 4)
    low, high = x == 0, x == 3
    turning = low | high
    level, levels = p // 8, n // 8
    ahead = (high & (level < levels - 2)) | (low & (level > 0) & (level < levels - 1))

    def near(dy):
        return (p, half * 4 + lax.rem(y + dy, 4))

    other_half = lax.rem(g + 4, 8)
    far = (p, other_half)
    next_p, last_p = lax.rem(p + 2, n), lax.rem(p + n - 2, n)
    after, before = (next_p, g), (last_p, g)
    twin = (p + 1 - 2 * core, g)
    closing_low, closing_high = low & (level == 0), high & (level == levels - 1)
    closing = closing_low | closing_high
    around = (jnp.where(low, last_p, next_p), other_half)
    across = (jnp.where(low, last_p, next_p), g)
    there = jnp.where(low, 3, 0)
    partners = [far, after, before, twin, near(1), near(2), near(3)]

    barrier = pltpu.get_barrier_semaphore()
    for device in partners:
        pl.semaphore_signal(barrier, inc=1, device_id=device, device_id_type=MESH)

    @pl.when(closing)
    def _():
        pl.semaphore_signal(barrier, inc=1, device_id=around, device_id_type=MESH)

    load_text = pltpu.make_async_copy(text_hbm, text_ref, load_sem.at[0])
    load_image = pltpu.make_async_copy(image_hbm, image_ref, load_sem.at[1])
    load_mask = pltpu.make_async_copy(mask_hbm, mask_ref, load_sem.at[2])
    load_neg = pltpu.make_async_copy(neg_hbm, neg_ref, load_sem.at[3])
    loads = [load_text, load_image, load_mask, load_neg]
    for load in loads:
        load.start()
    load_text.wait()
    normalize_rows(text_ref, text_mag, own, 0)
    load_mask.wait()
    load_neg.wait()
    lane = lax.broadcasted_iota(jnp.int32, (8, 128), 1)
    mine = (lane == neg_ref[0, 0]) | (lane == neg_ref[0, 1]) | (lane == g)
    tile = jnp.where(mine, 1.0, 0.0)
    for k in range(4):
        tile = jnp.where(lane == 8 + k, mask_ref[0, k].astype(jnp.float32), tile)
    tiles[OWN] = tile

    def slot_rows(slot):
        return pl.ds(pl.multiple_of(slot * (2 * rows), 2 * rows), 2 * rows)

    def piece(j, source):
        return pl.ds(pl.multiple_of(FAR * 2 * rows + j * (4 * part) + source * part, part), part)

    bit = part // 2

    def landing(i):
        first = FAR * 2 * rows + i // 2 * (4 * part) + lax.rem(i, 2) * bit
        return pl.ds(pl.multiple_of(first, bit), bit)

    def far_copy(i):
        return pltpu.make_async_remote_copy(
            src_ref=own.at[pl.ds(pl.multiple_of(i * bit, bit), bit)], dst_ref=held.at[landing(i)],
            send_sem=far_send.at[i], recv_sem=far_recv.at[i],
            device_id=far, device_id_type=MESH,
        )

    def slot_copy(i, src, slot, device):
        return pltpu.make_async_remote_copy(
            src_ref=src, dst_ref=held.at[slot_rows(slot)],
            send_sem=slot_send.at[i], recv_sem=slot_recv.at[slot],
            device_id=device, device_id_type=MESH,
        )

    def tile_copy(i, src_slot, slot, device):
        return pltpu.make_async_remote_copy(
            src_ref=tiles.at[src_slot], dst_ref=tiles.at[slot],
            send_sem=tile_send.at[i], recv_sem=tile_recv.at[slot],
            device_id=device, device_id_type=MESH,
        )

    def pass_copy(dy, j):
        return pltpu.make_async_remote_copy(
            src_ref=held.at[piece(j, 0)], dst_ref=held.at[piece(j, 4 - dy)],
            send_sem=pass_send.at[dy - 1, j], recv_sem=pass_recv.at[3 - dy, j],
            device_id=near(dy), device_id_type=MESH,
        )

    def back_copy(j):
        at = pl.ds(pl.multiple_of(j * part, part), part)
        return pltpu.make_async_remote_copy(
            src_ref=sent_back.at[at], dst_ref=got_back.at[at],
            send_sem=back_send.at[j], recv_sem=back_recv.at[j],
            device_id=far, device_id_type=MESH,
        )

    def edge_copy():
        first = pl.multiple_of(there * (2 * rows) + rows, rows)
        return pltpu.make_async_remote_copy(
            src_ref=own.at[pl.ds(rows, rows)], dst_ref=held.at[pl.ds(first, rows)],
            send_sem=edge_send, recv_sem=edge_recv,
            device_id=across, device_id_type=MESH,
        )

    def around_copy(j):
        first = pl.multiple_of(there * (2 * rows) + j * part, part)
        return pltpu.make_async_remote_copy(
            src_ref=held.at[piece(j, 0)], dst_ref=held.at[pl.ds(first, part)],
            send_sem=around_send.at[j], recv_sem=around_recv.at[j],
            device_id=around, device_id_type=MESH,
        )

    def closed():
        edge_copy().wait_recv()

        def came(j, carry):
            around_copy(j).wait_recv()
            return carry

        lax.fori_loop(0, PIECES, came, 0)

    pl.semaphore_wait(barrier, len(partners) + jnp.where(closing, 1, 0))

    def send_far(j, carry):
        far_copy(j).start()
        return carry


    @pl.when(ahead)
    def _():
        load_image.wait()
        normalize_rows(image_ref, image_mag, own, rows)

    @pl.when(ahead & high)
    def _():
        slot_copy(0, own, 0, after).start()

    @pl.when(ahead & low)
    def _():
        slot_copy(1, own, 3, before).start()

    lax.fori_loop(0, BITS, send_far, 0)


    @pl.when(jnp.logical_not(ahead))
    def _():
        load_image.wait()
        normalize_rows(image_ref, image_mag, own, rows)

    targets = [(after, 0), (before, 3), (twin, 1 + core)] + [(near(dy), OWN + 4 - dy) for dy in (1, 2, 3)]
    for i, (device, slot) in enumerate(targets):
        tile_copy(i, OWN, slot, device).start()
    for i in (3, 4, 5, 2):
        device, slot = targets[i]
        slot_copy(i, own, slot, device).start()

    @pl.when(jnp.logical_not(ahead & high))
    def _():
        slot_copy(0, own, 0, after).start()

    @pl.when(jnp.logical_not((ahead & low) | closing_low))
    def _():
        slot_copy(1, own, 3, before).start()

    @pl.when(closing_low)
    def _():
        edge_copy().start()

    held[slot_rows(OWN), :] = own[...]
    image_sum[...] = jnp.zeros_like(image_sum)
    text_sum[...] = jnp.zeros_like(text_sum)
    loss_sum[...] = jnp.zeros_like(loss_sum)

    source, place = 3 - 3 * core, 2 - core
    late = (low & (core == 1)) | (high & (core == 0))

    row = lax.broadcasted_iota(jnp.int32, (rows, rows), 0)
    column = lax.broadcasted_iota(jnp.int32, (rows, rows), 1)
    eye = jnp.where(row == column, 1.0, 0.0)
    first_lane = lax.broadcasted_iota(jnp.int32, (1, 128), 1)

    def weight(slot, index):
        picked = jnp.where(first_lane == index, tiles[slot, 0:1, :], 0.0)
        return jnp.sum(picked, axis=1, keepdims=True)

    def scores_of(own_block, other):
        return logit_scale * lax.dot_general(
            own_block, other, (((1,), (1,)), ((), ())), preferred_element_type=jnp.float32
        ) + logit_bias

    def sigmoid_of(scores):
        small = jnp.exp(-jnp.abs(scores))
        return jnp.where(scores >= 0.0, 1.0, small) / (1.0 + small)

    def image_side(other, w, diagonal):
        scores = scores_of(own[pl.ds(rows, rows), :], other)
        small = jnp.exp(-jnp.abs(scores))
        loss = jnp.maximum(scores, 0.0) + jnp.log1p(small)
        grad = jnp.where(scores >= 0.0, 1.0, small) / (1.0 + small)
        if diagonal is not None:
            loss = loss - diagonal * scores
            grad = grad - diagonal
        loss_sum[...] += w * loss
        image_sum[...] += jnp.dot(
            (w * grad).astype(jnp.bfloat16), other, preferred_element_type=jnp.float32
        )

    def text_side(other, w, diagonal):
        scores = scores_of(own[pl.ds(0, rows), :], other)
        text_sum[...] += jnp.dot(
            (w * (sigmoid_of(scores) - diagonal)).astype(jnp.bfloat16), other, preferred_element_type=jnp.float32
        )

    def unit(slot):
        in_loop = slot < 4
        group_index = half * 4 + lax.rem(y + slot, 4)
        diagonal = jnp.where(slot == OWN, 1.0, 0.0) * eye
        first = pl.multiple_of(slot * (2 * rows), 2 * rows)
        w = weight(OWN, jnp.where(in_loop, 8 + slot, group_index))
        image_side(held[pl.ds(first, rows), :], w, diagonal)
        w = weight(slot, jnp.where(in_loop, 11 - slot, g))
        text_side(held[pl.ds(first + rows, rows), :], w, diagonal)

    def far_weights():
        w = jnp.zeros((1, 128), jnp.float32)
        for r in range(4):
            w = jnp.where(first_lane // part == r, weight(OWN, (1 - half) * 4 + lax.rem(y + r, 4)), w)
            far_weight[r] = jnp.broadcast_to(weight(OWN + r, other_half), (8, 128))
        far_weight[4] = jnp.broadcast_to(w, (8, 128))

    def far_piece(k):
        first = pl.multiple_of(FAR * 2 * rows + k * (4 * part), 4 * part)
        return held[pl.ds(first, 4 * part), :]

    def arrived(k):
        for dy in (1, 2, 3):
            pass_copy(dy, k).wait_recv()

    def relay():
        @pl.when(late & closing_high)
        def _():
            closed()

        @pl.when(jnp.logical_not(late & closing_high))
        def _():
            slot_copy(6, held.at[slot_rows(source)], source, twin).wait_recv()

        slot_copy(6, held.at[slot_rows(source)], place, twin).start()
        tile_copy(6, source, source, twin).wait_recv()
        tile_copy(6, source, place, twin).start()

    def units(slot, carry):
        @pl.when((slot != OWN) & (slot != source))
        def _():
            @pl.when(closing_high & (slot == 3 - there))
            def _():
                closed()

            @pl.when(jnp.logical_not(closing_high & (slot == 3 - there)))
            def _():
                slot_copy(0, own, slot, after).wait_recv()

            tile_copy(0, OWN, slot, after).wait_recv()

        unit(slot)
        return carry

    @pl.when(jnp.logical_not(late))
    def _():
        relay()

    lax.fori_loop(OWN, OWN + 4, units, 0)
    far_weights()

    @pl.when(jnp.logical_not(turning))
    def _():
        lax.fori_loop(0, 4, units, 0)

    def step(j, carry):
        far_copy(2 * j).wait_recv()
        far_copy(2 * j + 1).wait_recv()
        for dy in (1, 2, 3):
            pass_copy(dy, j).start()

        @pl.when(closing_low)
        def _():
            around_copy(j).start()

        text_piece = held[piece(j, 0), :]
        total = jnp.zeros((part, image_ref.shape[1]), jnp.float32)
        for r in range(4):
            images = held[pl.ds((OWN + r) * 2 * rows + rows, rows), :]
            scores = scores_of(text_piece, images)
            grad = far_weight[r, 0:1, :] * sigmoid_of(scores)
            total += jnp.dot(grad.astype(jnp.bfloat16), images, preferred_element_type=jnp.float32)
        sent_back[pl.ds(pl.multiple_of(j * part, part), part), :] = total.astype(jnp.bfloat16)
        back_copy(j).start()

        @pl.when(j >= LAG)
        def _():
            far_image(j - LAG)

        return carry

    def far_image(k):
        arrived(k)
        image_side(far_piece(k), far_weight[4, 0:1, :], None)

    lax.fori_loop(0, PIECES, step, 0)

    for k in range(PIECES - LAG, PIECES):
        far_image(k)

    @pl.when(turning)
    def _():
        def turned(t, carry):
            @pl.when((t == 3) & late)
            def _():
                relay()

            turn = jnp.where((t < 2) | late, t, 5 - t)
            return units(jnp.where(low, 3 - turn, turn), carry)

        lax.fori_loop(0, 4, turned, 0)

    loss_ref[...] = jnp.sum(loss_sum[...].T, axis=0, keepdims=True)
    backward_rows(image_ref, image_mag, image_sum, None, image_out, 0, rows)

    def finish(j, carry):
        back_copy(j).wait_recv()
        backward_rows(text_ref, text_mag, text_sum, got_back, text_out, j * part, part)
        return carry

    lax.fori_loop(0, PIECES, finish, 0)

    for i, (device, slot) in enumerate(targets):
        tile_copy(i, OWN, slot, device).wait_send()
        if i >= 2:
            slot_copy(i, own, slot, device).wait_send()

    slot_copy(0, own, 0, after).wait_send()

    @pl.when(jnp.logical_not(closing_low))
    def _():
        slot_copy(1, own, 3, before).wait_send()

    @pl.when(closing_low)
    def _():
        edge_copy().wait_send()

    tile_copy(6, source, place, twin).wait_send()
    slot_copy(6, held.at[slot_rows(source)], place, twin).wait_send()

    def sent(j, carry):
        for dy in (1, 2, 3):
            pass_copy(dy, j).wait_send()
        far_copy(2 * j).wait_send()
        far_copy(2 * j + 1).wait_send()
        back_copy(j).wait_send()

        @pl.when(closing_low)
        def _():
            around_copy(j).wait_send()

        return carry

    lax.fori_loop(0, PIECES, sent, 0)


def on_device(image_emb, text_emb, loop_mask, neg_list):
    rows, width = image_emb.shape
    vmem = pl.BlockSpec(memory_space=pltpu.VMEM)
    hbm = pl.BlockSpec(memory_space=pltpu.HBM)
    losses, image_grad, text_grad = pl.pallas_call(
        kernel,
        out_shape=(
            jax.ShapeDtypeStruct((1, rows), jnp.float32),
            jax.ShapeDtypeStruct((rows, width), jnp.bfloat16),
            jax.ShapeDtypeStruct((rows, width), jnp.bfloat16),
        ),
        in_specs=[hbm] * 4,
        out_specs=(vmem, vmem, vmem),
        scratch_shapes=[
            pltpu.VMEM((rows, width), jnp.bfloat16),
            pltpu.VMEM((rows, width), jnp.bfloat16),
            pltpu.SMEM(loop_mask.shape, jnp.int32),
            pltpu.SMEM(neg_list.shape, jnp.int32),
            pltpu.VMEM((2 * rows, width), jnp.bfloat16),
            pltpu.VMEM((FAR * 2 * rows + 4 * rows, width), jnp.bfloat16),
            pltpu.VMEM((8, 8, 128), jnp.float32),
            pltpu.VMEM((rows, 1), jnp.float32),
            pltpu.VMEM((rows, 1), jnp.float32),
            pltpu.VMEM((rows, width), jnp.float32),
            pltpu.VMEM((rows, width), jnp.float32),
            pltpu.VMEM((rows, rows), jnp.float32),
            pltpu.VMEM((5, 8, 128), jnp.float32),
            pltpu.VMEM((rows, width), jnp.bfloat16),
            pltpu.VMEM((rows, width), jnp.bfloat16),
            pltpu.SemaphoreType.DMA((4,)),
            pltpu.SemaphoreType.DMA((BITS,)),
            pltpu.SemaphoreType.DMA((BITS,)),
            pltpu.SemaphoreType.DMA((7,)),
            pltpu.SemaphoreType.DMA((8,)),
            pltpu.SemaphoreType.DMA((7,)),
            pltpu.SemaphoreType.DMA((8,)),
            pltpu.SemaphoreType.DMA((3, PIECES)),
            pltpu.SemaphoreType.DMA((3, PIECES)),
            pltpu.SemaphoreType.DMA((PIECES,)),
            pltpu.SemaphoreType.DMA((PIECES,)),
            pltpu.SemaphoreType.DMA,
            pltpu.SemaphoreType.DMA,
            pltpu.SemaphoreType.DMA((PIECES,)),
            pltpu.SemaphoreType.DMA((PIECES,)),
        ],
        compiler_params=pltpu.CompilerParams(
            collective_id=0, has_side_effects=True, vmem_limit_bytes=60 * 2**20
        ),
        name="pair_blocks",
    )(image_emb, text_emb, loop_mask, neg_list)
    return losses.reshape(rows), image_grad, text_grad


def solution(mesh):
    placed = (
        P(("blk", "grp"), None),
        P(("blk", "grp"), None),
        P(("blk", "grp"), None),
        P(("blk", "grp"), None),
    )
    return jax.shard_map(
        on_device,
        mesh=mesh,
        in_specs=placed,
        out_specs=(P(("blk", "grp")), P(("blk", "grp"), None), P(("blk", "grp"), None)),
        check_vma=False,
    )
```
